32 devices in a mesh: groups: 2 (over x), ctx: 16 (over z, y, core).
Axes of the slice: x: 2, y: 2, z: 4, core: 2. Of those that a mesh axis runs over, the one named last changes fastest.
Arguments:
- queries: bfloat16 [4096, 4096], P(('groups', 'ctx')), parts along dimension 0, may hold values from -5 to 5
- keys: bfloat16 [3, 4096, 1024], P(None, ('groups', 'ctx')), parts along dimension 1, may hold values from -5 to 5
- values: bfloat16 [3, 4096, 1024], P(None, ('groups', 'ctx')), parts along dimension 1, may hold values from -5 to 5
- picks: int32 [32, 8, 2], P(('groups', 'ctx')), parts along dimension 0, may hold values from 1 to 15, as said below
Outputs:
- attended: bfloat16 [4096, 4096], P(('groups', 'ctx')), parts along dimension 0
The draws below stay inside these ranges and needn't reach their ends.
There are 2 independent parts, one for each index of `groups`. The reference program is written for one: setup_inputs(seed, part) draws one part's arguments, and reference() takes and returns one part's arrays. A program takes and returns all parts, laid end to end along the dimension named above; each array names one. Nothing has to cross between parts.
Inputs may be any that keep to these rules, and one draw needn't show every extreme that they name: `picks`: each entry is a block before the query's own block and never block 0. Rows 2q and 2q + 1 are equal (one query block). The 2 entries of one head differ in (entry mod 8); within a row no value of (entry mod 8) occurs more than 2 times, and one occurs exactly 2 times.
All inputs are finite; a program needn't handle non-finite values.
Results may differ from the reference program's by a relative error of at most 0.0048.
Values may be sent and summed in bfloat16 or wider, within the bound.
A program may use at most 64 MiB of HBM per device.

```python
import jax
import jax.numpy as jnp
from jax import lax

BLK = 256
HALF = 128
HD = 128
KVH = 8
QH = 32
GRP = 4
FURTHER = 2
KVB_DEV = 3
PAIRS = 8
ROWS_ALL = 2048
N_CTX = 16


def draw_queries(key, part):
    key = jax.random.fold_in(key, 12)
    drawn = jnp.clip(jax.random.normal(key, (ROWS_ALL, QH * HD), jnp.float32), -5.0, 5.0)
    return drawn.astype(jnp.bfloat16)


def draw_keys(key, part):
    key = jax.random.fold_in(key, 11)
    drawn = jnp.clip(jax.random.normal(key, (KVB_DEV, ROWS_ALL, KVH * HD), jnp.float32), -5.0, 5.0)
    return drawn.astype(jnp.bfloat16)


def spread_pairs(order):
    wanted = FURTHER * KVH
    copies = (wanted + PAIRS - 1) // PAIRS
    return jnp.concatenate([jnp.roll(order, -shift) for shift in range(copies)])[:wanted]


def draw_picks(key, part):
    key = jax.random.fold_in(key, 13)
    hot_key, each_key, flag_key, row_key, hot_row_key, fix_key = jax.random.split(key, 6)
    first_key = jax.random.fold_in(key, 7)
    wanted = FURTHER * KVH
    hot_pairs = spread_pairs(jax.random.permutation(hot_key, PAIRS))
    each_pairs = jax.vmap(lambda sub_key: spread_pairs(jax.random.permutation(sub_key, PAIRS)))(jax.random.split(each_key, PAIRS))
    popular = jax.random.randint(flag_key, (PAIRS, 1), 0, 4) < 3
    pair_ids = jnp.where(popular, hot_pairs[None, :], each_pairs)
    hot_rows = jax.random.randint(hot_row_key, (wanted,), 0, KVB_DEV - 1)
    drawn_rows = jax.random.randint(row_key, (PAIRS, wanted), 0, KVB_DEV - 1)
    row_ids = jnp.where(popular, hot_rows[None, :], drawn_rows)
    shuffled = jax.random.permutation(first_key, PAIRS)
    order_keys = jnp.where(shuffled == PAIRS - 1, 0, jnp.where(shuffled == 1, 1, 2))
    ordered = shuffled[jnp.argsort(order_keys, stable=True)]
    pair_ids = pair_ids.at[0].set(spread_pairs(ordered))
    first_rows = row_ids[0].at[0].set(KVB_DEV - 2).at[1].set(0)
    row_ids = row_ids.at[0].set(first_rows)
    moved_rows = jax.random.randint(fix_key, (PAIRS, wanted), 1, KVB_DEV - 1)
    row_ids = jnp.where((pair_ids == 0) & (row_ids == 0), moved_rows, row_ids)
    blocks = (row_ids * PAIRS + pair_ids).reshape(PAIRS, KVH, FURTHER)
    return jnp.repeat(blocks, 2, axis=0).astype(jnp.int32)


def steps_of(key, shape, cuts, low, high):
    def one(dim, blocks):
        heights = jax.random.uniform(jax.random.fold_in(jax.random.fold_in(key, 6), dim), (blocks,), jnp.float32, low / len(cuts), high / len(cuts))
        return jnp.repeat(jnp.exp(heights), shape[dim] // blocks).reshape((-1,) + (1,) * (len(shape) - dim - 1))

    level = one(*cuts[0])
    for cut in cuts[1:]:
        level = level * one(*cut)
    return level


def noise(key, shape, deviation, bound, shards=(), kind=jnp.bfloat16):
    values = jax.random.normal(key, shape, jnp.float32) * deviation
    if len(shards) > 0:
        values = steps_of(key, shape, shards, -0.22, 0.18) * values
    return jnp.clip(values, min=-bound, max=bound).astype(kind)


def setup_inputs(seed: int = 0, part: int = 0) -> dict:
    key_list = jax.random.split(jax.random.key(seed), 5)
    part_splits = jax.random.split(jax.random.fold_in(key_list[4], part), 5)
    return {
        "queries": draw_queries(jax.random.fold_in(jax.random.fold_in(key_list[4], part), 71), part),
        "keys": draw_keys(jax.random.fold_in(jax.random.fold_in(key_list[4], part), 71), part),
        "values": noise(part_splits[2], (KVB_DEV, ROWS_ALL, KVH * HD), 1.0, 5.0, ((1, 16),)),
        "picks": draw_picks(jax.random.fold_in(jax.random.fold_in(key_list[4], part), 71), part),
    }


def attend(query_rows, key_cat, value_cat, usable):
    score_scale = HD ** -0.5
    grouped = query_rows.reshape(HALF, KVH, GRP, HD).astype(jnp.float32)
    results = []
    for kv_head in range(KVH):
        scores = jnp.einsum("tgd,kd->gtk", grouped[:, kv_head], key_cat[kv_head].astype(jnp.float32)) * score_scale
        scores = jnp.where(usable[None], scores, -jnp.inf)
        highest = jnp.max(scores, axis=-1, keepdims=True)
        weights = jnp.exp(scores - highest)
        totals = jnp.sum(weights, axis=-1)
        rounded = lax.optimization_barrier(weights.astype(jnp.bfloat16)).astype(jnp.float32)
        blended = jnp.einsum("gtk,kd->tgd", rounded, value_cat[kv_head].astype(jnp.float32))
        results.append(blended / totals.T[:, :, None])
    return jnp.stack(results, axis=1).reshape(HALF, QH * HD).astype(jnp.bfloat16)


def key_mask(odd_half):
    picked_end = (1 + FURTHER) * BLK
    own_start = picked_end + HALF
    columns = jnp.arange(own_start + HALF)[None, :]
    query_pos = jnp.arange(HALF)[:, None]
    before = columns < picked_end
    earlier = (columns >= picked_end) & (columns < own_start) & odd_half
    causal = (columns >= own_start) & (columns - own_start <= query_pos)
    return before | earlier | causal


def reference(queries, keys, values, picks):
    key_rows = keys.reshape(KVB_DEV, N_CTX, HALF, KVH, HD)
    value_rows = values.reshape(KVB_DEV, N_CTX, HALF, KVH, HD)

    def block_of(cache_rows, block_id):
        row_index = block_id // PAIRS
        pair_index = block_id % PAIRS
        return jnp.concatenate([cache_rows[row_index, 2 * pair_index], cache_rows[row_index, 2 * pair_index + 1]], axis=0)

    def one_half(device):
        query_rows = lax.dynamic_slice_in_dim(queries, device * HALF, HALF, 0)

        def assemble(cache_rows):
            leading = block_of(cache_rows, jnp.int32(0))
            earlier = cache_rows[KVB_DEV - 1, jnp.maximum(device - 1, 0)]
            own_half = cache_rows[KVB_DEV - 1, device]
            head_list = []
            for kv_head in range(KVH):
                chosen = [block_of(cache_rows, picks[device, kv_head, slot])[:, kv_head] for slot in range(FURTHER)]
                head_list.append(jnp.concatenate([leading[:, kv_head]] + chosen + [earlier[:, kv_head], own_half[:, kv_head]], axis=0))
            return jnp.stack(head_list, axis=0)

        usable = key_mask(device % 2 == 1)
        return attend(query_rows, assemble(key_rows), assemble(value_rows), usable)

    stacked = lax.map(one_half, jnp.arange(N_CTX, dtype=jnp.int32))
    return stacked.reshape(ROWS_ALL, QH * HD)
```

```python
import functools
import math

import jax
import jax.numpy as jnp
from jax import lax
from jax.experimental import pallas as pl
from jax.experimental.pallas import tpu as pltpu
from jax.sharding import PartitionSpec as P

HD = 128
KVH = 8
GRP = 4
FURTHER = 2
WANTED = KVH * FURTHER
CHUNKS = 4
MESH = pl.DeviceIdType.MESH
SCALE = HD ** -0.5
EXP2_SCALE = SCALE * math.log2(math.e)


def xor_of(a, b, n):
    a, b = jnp.int32(a), jnp.int32(b)
    total = 0
    bit = 1
    while bit < n:
        total = total + lax.rem(lax.rem(lax.div(a, bit), 2) + lax.rem(lax.div(b, bit), 2), 2) * bit
        bit *= 2
    return total


def partial_attend(rows, keys, values, usable=None):
    scores = lax.dot_general(
        rows, keys, (((1,), (1,)), ((), ())), preferred_element_type=jnp.float32
    )
    if usable is not None:
        scores = jnp.where(usable, scores, -jnp.inf)
    highest = jnp.max(scores, axis=-1, keepdims=True)
    weights = jnp.exp2((scores - highest) * EXP2_SCALE)
    total = jnp.sum(weights, axis=-1, keepdims=True)
    blended = jnp.dot(
        weights.astype(jnp.bfloat16), values, preferred_element_type=jnp.float32
    )
    return blended, highest, total


def kernel(
    n, slots, picks_ref, q_hbm, k_hbm, v_hbm, o_hbm,
    qv, kv, vv, blk, earl, pk, pk_sm, send, recv,
    acc_l, max_l, tot_l, acc_p, max_p, tot_p, stage,
    load_sem, q_sem, root_sem, earl_loc, earl_s, earl_r, pk_s, pk_r, sm_sem,
    blk_s, blk_r, a2a_s, a2a_r, fwd_s, fwd_r, out_sem,
):
    me = lax.axis_index("ctx")
    chip, core = me // 2, me % 2
    z, y = chip // 2, chip % 2
    depth = n // 2
    half = q_hbm.shape[0]
    last = k_hbm.shape[0] - 1
    sibling = chip * 2 + 1 - core

    def peer(k):
        return xor_of(chip, k, n) * 2 + core

    def remote(src, dst, s_sem, r_sem, dest):
        return pltpu.make_async_remote_copy(
            src_ref=src, dst_ref=dst, send_sem=s_sem, recv_sem=r_sem,
            device_id={"ctx": dest}, device_id_type=MESH,
        )

    def cache_loads(head):
        window = pl.ds(pl.multiple_of(head * HD, HD), HD)
        return [
            pltpu.make_async_copy(src.at[row, :, window], dst.at[row * KVH + head], load_sem.at[i, row, head])
            for i, (src, dst) in enumerate(((k_hbm, kv), (v_hbm, vv)))
            for row in range(last + 1)
        ]

    def query_load(head, g):
        window = pl.ds(pl.multiple_of((head * GRP + g) * HD, HD), HD)
        return pltpu.make_async_copy(q_hbm.at[:, window], qv.at[head, pl.ds(g * half, half)], q_sem.at[head, g])

    root_loads = [
        pltpu.make_async_copy(src.at[0], blk.at[core, i], root_sem.at[i])
        for i, src in enumerate((k_hbm, v_hbm))
    ]

    @pl.when(chip == 0)
    def _():
        for copy in root_loads:
            copy.start()

    def load_cache(head, carry):
        for copy in cache_loads(head):
            copy.start()
        return carry

    lax.fori_loop(0, KVH, load_cache, 0)

    barrier = pltpu.get_barrier_semaphore()

    def greet(k, carry):
        pl.semaphore_signal(barrier, inc=1, device_id={"ctx": peer(k)}, device_id_type=MESH)
        return carry

    lax.fori_loop(1, n, greet, 0)
    pl.semaphore_signal(barrier, inc=1, device_id={"ctx": sibling}, device_id_type=MESH)

    lanes = lax.broadcasted_iota(jnp.int32, (KVH, HD), 1)
    subs = lax.broadcasted_iota(jnp.int32, (KVH, HD), 0)
    mine = picks_ref[0]
    spread = jnp.where(lanes == subs, mine[:, 0:1], 0)
    spread = spread + jnp.where(lanes == subs + KVH, mine[:, 1:2], 0)
    pk[0] = jnp.sum(spread, axis=0, keepdims=True)

    pl.semaphore_wait(barrier, n)

    def pk_copy(k):
        return remote(pk.at[0], pk.at[k], pk_s.at[k], pk_r.at[k], peer(k))

    def pk_send(k, carry):
        pk_copy(k).start()
        return carry

    lax.fori_loop(1, n, pk_send, 0)

    rows_of = half // (CHUNKS // 2)

    def blk_part(side, ch):
        return blk.at[side, ch // (CHUNKS // 2), pl.ds((ch % (CHUNKS // 2)) * rows_of, rows_of)]

    column = y == core
    routes = [
        (column & (z == 0), (2 + y) * 2 + core),
        (column & (z >= 2) & (z + 1 < depth), ((z + 1) * 2 + y) * 2 + core),
        (column & jnp.logical_not((core == 1) & (z == 0)), (z * 2 + 1 - y) * 2 + core),
        ((chip == 0) & (core == 1), 3),
    ]
    if depth > 2:
        routes.append((column & (z == 0), (4 + y) * 2 + core))

    def blk_copy(kind, ch):
        return remote(
            blk_part(core, ch), blk_part(core, ch), blk_s.at[kind, ch], blk_r.at[0, ch], routes[kind][1]
        )

    def blk_sib(ch):
        return remote(
            blk_part(core, ch), blk_part(core, ch), blk_s.at[len(routes), ch], blk_r.at[1, ch], sibling
        )

    def blk_start(ch):
        for kind, (wanted, _) in enumerate(routes):
            @pl.when(wanted)
            def _():
                blk_copy(kind, ch).start()
        blk_sib(ch).start()

    @pl.when(chip == 0)
    def _():
        for copy in root_loads:
            copy.wait()
        for ch in range(CHUNKS):
            blk_start(ch)

    earl_copies = [
        remote(src.at[last], earl.at[i], earl_s.at[i], earl_r.at[i], sibling)
        for i, src in enumerate((k_hbm, v_hbm))
    ]
    earl_locals = [
        pltpu.make_async_copy(src.at[last], earl.at[i], earl_loc.at[i])
        for i, src in enumerate((k_hbm, v_hbm))
    ]

    @pl.when(core == 0)
    def _():
        for copy in earl_copies + earl_locals:
            copy.start()

    def load_queries(head, carry):
        for g in range(GRP):
            query_load(head, g).start()
        return carry

    lax.fori_loop(0, KVH, load_queries, 0)

    def wait_cache(head, carry):
        for copy in cache_loads(head):
            copy.wait()
        return carry

    lax.fori_loop(0, KVH, wait_cache, 0)

    def pk_wait(k, carry):
        pk_copy(k).wait_recv()
        return carry

    lax.fori_loop(1, n, pk_wait, 0)
    to_scalar = pltpu.make_async_copy(pk, pk_sm, sm_sem)
    to_scalar.start()
    to_scalar.wait()

    def served(k, pair):
        found = [(jnp.int32(0), jnp.int32(0))] * slots
        count = jnp.int32(0)
        for e in range(WANTED):
            block = pk_sm[k, 0, e]
            match = lax.rem(block, n) == pair
            for m in range(slots):
                hit = match & (count == m)
                head, row = found[m]
                found[m] = (jnp.where(hit, e % KVH, head), jnp.where(hit, lax.div(block, n), row))
            count = count + match.astype(jnp.int32)
        return found

    def gather(k, dst):
        for m, (head, row) in enumerate(served(k, chip)):
            dst[m, 0] = kv[row * KVH + head]
            dst[m, 1] = vv[row * KVH + head]

    def a2a_copy(k):
        return remote(send.at[k], recv.at[k, core], a2a_s.at[k], a2a_r.at[k], peer(k))

    def a2a_send(i, carry):
        k = n - 1 - i
        gather(k, send.at[k])
        a2a_copy(k).start()
        return carry

    lax.fori_loop(0, n - 1, a2a_send, 0)
    gather(0, recv.at[0, core])

    def fwd_copy(k):
        return remote(recv.at[k, core], recv.at[k, core], fwd_s.at[k], fwd_r.at[k], sibling)

    fwd_copy(0).start()

    @pl.when(chip != 0)
    def _():
        for ch in range(CHUNKS):
            blk_copy(0, ch).wait_recv()
            blk_start(ch)

    def wait_queries(head, carry):
        for g in range(GRP):
            query_load(head, g).wait()
        return carry

    lax.fori_loop(0, KVH, wait_queries, 0)

    @pl.when(core == 0)
    def _():
        for copy in earl_locals:
            copy.wait()

    @pl.when(core == 1)
    def _():
        for copy in earl_copies:
            copy.wait_recv()

    for ch in range(CHUNKS):
        blk_sib(ch).wait_recv()

    def local_head(head, carry):
        window = pl.ds(pl.multiple_of(head * HD, HD), HD)
        keys = jnp.concatenate(
            [blk[0, 0, :, window], blk[1, 0, :, window], earl[0, :, window], kv[last * KVH + head]], axis=0
        )
        values = jnp.concatenate(
            [blk[0, 1, :, window], blk[1, 1, :, window], earl[1, :, window], vv[last * KVH + head]], axis=0
        )
        shape = (GRP * half, 4 * half)
        columns = lax.broadcasted_iota(jnp.int32, shape, 1)
        query_pos = lax.broadcasted_iota(jnp.int32, shape, 0) % half
        usable = columns < 2 * half + half * core
        usable = usable | ((columns >= 3 * half) & (columns - 3 * half <= query_pos))
        blended, highest, total = partial_attend(qv[head], keys, values, usable)
        acc_l[head] = blended
        max_l[head] = highest
        tot_l[head] = total
        return carry

    lax.fori_loop(0, KVH, local_head, 0)

    def picked(k):
        for m, (head, _) in enumerate(served(0, xor_of(chip, k, n))):
            keys = jnp.concatenate([recv[k, 0, m, 0], recv[k, 1, m, 0]], axis=0)
            values = jnp.concatenate([recv[k, 0, m, 1], recv[k, 1, m, 1]], axis=0)
            blended, highest, total = partial_attend(qv[head], keys, values)
            acc_p[k * slots + m] = blended
            max_p[k * slots + m] = highest
            tot_p[k * slots + m] = total

    def forward(k):
        a2a_copy(k).wait_recv()
        fwd_copy(k).start()

    def sib_wait(k):
        remote(
            recv.at[k, 1 - core], recv.at[k, 1 - core], fwd_s.at[k], fwd_r.at[k], sibling
        ).wait_recv()

    def step(i, carry):
        k = (n - i) % n
        forward(n - 1 - i)
        sib_wait(k)
        picked(k)
        return carry

    lax.fori_loop(0, n - 1, step, 0)
    sib_wait(1)
    picked(1)

    def out_copy(head):
        window = pl.ds(pl.multiple_of(head * GRP * HD, GRP * HD), GRP * HD)
        return pltpu.make_async_copy(stage.at[:, window], o_hbm.at[:, window], out_sem.at[head])

    def merge(head, carry):
        parts = [(acc_l[head], max_l[head], tot_l[head])]
        for s in range(FURTHER):
            entry = s * KVH + head
            pair = lax.rem(pk_sm[0, 0, entry], n)
            rank = jnp.int32(0)
            for e in range(WANTED):
                same = (lax.rem(pk_sm[0, 0, e], n) == pair) & (e < entry)
                rank = rank + same.astype(jnp.int32)
            index = xor_of(pair, chip, n) * slots + jnp.minimum(rank, slots - 1)
            parts.append((acc_p[index], max_p[index], tot_p[index]))
        top = functools.reduce(jnp.maximum, [part[1] for part in parts])
        shares = [jnp.exp2((part[1] - top) * EXP2_SCALE) for part in parts]
        total = sum(share * part[2] for share, part in zip(shares, parts))
        result = sum((share / total) * part[0] for share, part in zip(shares, parts))
        result = result.astype(stage.dtype)
        for g in range(GRP):
            window = pl.ds(pl.multiple_of((head * GRP + g) * HD, HD), HD)
            stage[:, window] = result[g * half:(g + 1) * half]
        out_copy(head).start()
        return carry

    lax.fori_loop(0, KVH, merge, 0)

    def drain(k, carry):
        pk_copy(k).wait_send()
        a2a_copy(k).wait_send()
        return carry

    lax.fori_loop(1, n, drain, 0)

    def drain_fwd(k, carry):
        fwd_copy(k).wait_send()
        return carry

    lax.fori_loop(0, n, drain_fwd, 0)
    for ch in range(CHUNKS):
        for kind, (wanted, _) in enumerate(routes):
            @pl.when(wanted)
            def _():
                blk_copy(kind, ch).wait_send()
        blk_sib(ch).wait_send()

    @pl.when(core == 0)
    def _():
        for copy in earl_copies:
            copy.wait_send()

    def drain_out(head, carry):
        out_copy(head).wait()
        return carry

    lax.fori_loop(0, KVH, drain_out, 0)


def solution(mesh):
    n = mesh.shape["ctx"] // 2
    slots = (WANTED + n - 1) // n
    bf16, f32 = jnp.bfloat16, jnp.float32

    def shard(queries, keys, values, picks):
        half, width = queries.shape
        rows = keys.shape[0]
        kv_width = keys.shape[2]
        dma = pltpu.SemaphoreType.DMA
        anywhere = pl.BlockSpec(memory_space=pl.ANY)
        return pl.pallas_call(
            functools.partial(kernel, n, slots),
            out_shape=jax.ShapeDtypeStruct(queries.shape, bf16),
            in_specs=[pl.BlockSpec(memory_space=pltpu.VMEM), anywhere, anywhere, anywhere],
            out_specs=anywhere,
            scratch_shapes=[
                pltpu.VMEM((KVH, GRP * half, HD), bf16),
                pltpu.VMEM((rows * KVH, half, HD), bf16),
                pltpu.VMEM((rows * KVH, half, HD), bf16),
                pltpu.VMEM((2, 2, half, kv_width), bf16),
                pltpu.VMEM((2, half, kv_width), bf16),
                pltpu.VMEM((n, 1, HD), jnp.int32),
                pltpu.SMEM((n, 1, HD), jnp.int32),
                pltpu.VMEM((n, slots, 2, half, HD), bf16),
                pltpu.VMEM((n, 2, slots, 2, half, HD), bf16),
                pltpu.VMEM((KVH, GRP * half, HD), f32),
                pltpu.VMEM((KVH, GRP * half, 1), f32),
                pltpu.VMEM((KVH, GRP * half, 1), f32),
                pltpu.VMEM((n * slots, GRP * half, HD), f32),
                pltpu.VMEM((n * slots, GRP * half, 1), f32),
                pltpu.VMEM((n * slots, GRP * half, 1), f32),
                pltpu.VMEM((half, width), bf16),
                dma((2, rows, KVH)), dma((KVH, GRP)), dma((2,)), dma((2,)), dma((2,)), dma((2,)),
                dma((n,)), dma((n,)), dma,
                dma((6, CHUNKS)), dma((2, CHUNKS)),
                dma((n,)), dma((n,)), dma((n,)), dma((n,)), dma((KVH,)),
            ],
            compiler_params=pltpu.CompilerParams(
                collective_id=0, has_side_effects=True, vmem_limit_bytes=56 * 2**20
            ),
        )(picks, queries, keys, values)

    placed = (
        P(("groups", "ctx"), None),
        P(None, ("groups", "ctx"), None),
        P(None, ("groups", "ctx"), None),
        P(("groups", "ctx"), None, None),
    )
    return jax.shard_map(
        shard, mesh=mesh, in_specs=placed, out_specs=P(("groups", "ctx"), None), check_vma=False
    )
```

```python
import functools
import math

import jax
import jax.numpy as jnp
from jax import lax
from jax.experimental import pallas as pl
from jax.experimental.pallas import tpu as pltpu
from jax.sharding import PartitionSpec as P

HD = 128
KVH = 8
GRP = 4
FURTHER = 2
WANTED = KVH * FURTHER
CHUNKS = 4
MESH = pl.DeviceIdType.MESH
SCALE = HD ** -0.5
EXP2_SCALE = SCALE * math.log2(math.e)


def xor_of(a, b, n):
    a, b = jnp.int32(a), jnp.int32(b)
    total = 0
    bit = 1
    while bit < n:
        total = total + lax.rem(lax.rem(lax.div(a, bit), 2) + lax.rem(lax.div(b, bit), 2), 2) * bit
        bit *= 2
    return total


def partial_attend(rows, keys, values, usable=None):
    scores = lax.dot_general(
        rows, keys, (((1,), (1,)), ((), ())), preferred_element_type=jnp.float32
    )
    if usable is not None:
        scores = jnp.where(usable, scores, -jnp.inf)
    highest = jnp.max(scores, axis=-1, keepdims=True)
    weights = jnp.exp2((scores - highest) * EXP2_SCALE)
    total = jnp.sum(weights, axis=-1, keepdims=True)
    blended = jnp.dot(
        weights.astype(jnp.bfloat16), values, preferred_element_type=jnp.float32
    )
    return blended, highest, total


def kernel(
    n, slots, picks_hbm, q_hbm, k_hbm, v_hbm, o_hbm,
    own_picks, qv, kv, vv, blk, earl, pk, pk_sm, send, recv,
    acc_l, max_l, tot_l, acc_p, max_p, tot_p, stage,
    load_sem, q_sem, root_sem, earl_loc, earl_s, earl_r, pk_s, pk_r, sm_sem,
    blk_s, blk_r, a2a_s, a2a_r, fwd_s, fwd_r, out_sem,
):
    me = lax.axis_index("ctx")
    chip, core = me // 2, me % 2
    z, y = chip // 2, chip % 2
    depth = n // 2
    half = q_hbm.shape[0]
    last = k_hbm.shape[0] - 1
    sibling = chip * 2 + 1 - core

    def peer(k):
        return xor_of(chip, k, n) * 2 + core

    def remote(src, dst, s_sem, r_sem, dest):
        return pltpu.make_async_remote_copy(
            src_ref=src, dst_ref=dst, send_sem=s_sem, recv_sem=r_sem,
            device_id={"ctx": dest}, device_id_type=MESH,
        )

    def cache_loads(head):
        window = pl.ds(pl.multiple_of(head * HD, HD), HD)
        return [
            pltpu.make_async_copy(src.at[row, :, window], dst.at[row * KVH + head], load_sem.at[i, row, head])
            for i, (src, dst) in enumerate(((k_hbm, kv), (v_hbm, vv)))
            for row in range(last + 1)
        ]

    def query_load(head, g):
        window = pl.ds(pl.multiple_of((head * GRP + g) * HD, HD), HD)
        return pltpu.make_async_copy(q_hbm.at[:, window], qv.at[head, pl.ds(g * half, half)], q_sem.at[head, g])

    root_loads = [
        pltpu.make_async_copy(src.at[0], blk.at[core, i], root_sem.at[i])
        for i, src in enumerate((k_hbm, v_hbm))
    ]

    picks_load = pltpu.make_async_copy(picks_hbm, own_picks, sm_sem.at[1])
    picks_load.start()

    @pl.when(chip == 0)
    def _():
        for copy in root_loads:
            copy.start()

    def load_cache(head, carry):
        for copy in cache_loads(head):
            copy.start()
        return carry

    lax.fori_loop(0, KVH, load_cache, 0)

    barrier = pltpu.get_barrier_semaphore()

    def greet(k, carry):
        pl.semaphore_signal(barrier, inc=1, device_id={"ctx": peer(k)}, device_id_type=MESH)
        return carry

    lax.fori_loop(1, n, greet, 0)
    pl.semaphore_signal(barrier, inc=1, device_id={"ctx": sibling}, device_id_type=MESH)

    lanes = lax.broadcasted_iota(jnp.int32, (KVH, HD), 1)
    subs = lax.broadcasted_iota(jnp.int32, (KVH, HD), 0)
    picks_load.wait()
    mine = own_picks[0]
    spread = jnp.where(lanes == subs, mine[:, 0:1], 0)
    spread = spread + jnp.where(lanes == subs + KVH, mine[:, 1:2], 0)
    pk[0] = jnp.sum(spread, axis=0, keepdims=True)

    pl.semaphore_wait(barrier, n)

    def pk_copy(k):
        return remote(pk.at[0], pk.at[k], pk_s.at[k], pk_r.at[k], peer(k))

    def pk_send(k, carry):
        pk_copy(k).start()
        return carry

    lax.fori_loop(1, n, pk_send, 0)

    rows_of = half // (CHUNKS // 2)

    def blk_part(side, ch):
        return blk.at[side, ch // (CHUNKS // 2), pl.ds((ch % (CHUNKS // 2)) * rows_of, rows_of)]

    column = y == core
    routes = [
        (column & (z + 1 < depth), ((z + 1) * 2 + y) * 2 + core),
        (column & jnp.logical_not((core == 1) & (z == 0)), (z * 2 + 1 - y) * 2 + core),
        ((chip == 0) & (core == 1), 3),
    ]

    def blk_copy(kind, ch):
        return remote(
            blk_part(core, ch), blk_part(core, ch), blk_s.at[kind, ch], blk_r.at[0, ch], routes[kind][1]
        )

    def blk_sib(ch):
        return remote(
            blk_part(core, ch), blk_part(core, ch), blk_s.at[len(routes), ch], blk_r.at[1, ch], sibling
        )

    def blk_start(ch):
        for kind, (wanted, _) in enumerate(routes):
            @pl.when(wanted)
            def _():
                blk_copy(kind, ch).start()
        blk_sib(ch).start()

    @pl.when(chip == 0)
    def _():
        for copy in root_loads:
            copy.wait()
        for ch in range(CHUNKS):
            blk_start(ch)

    earl_copies = [
        remote(src.at[last], earl.at[i], earl_s.at[i], earl_r.at[i], sibling)
        for i, src in enumerate((k_hbm, v_hbm))
    ]
    earl_locals = [
        pltpu.make_async_copy(src.at[last], earl.at[i], earl_loc.at[i])
        for i, src in enumerate((k_hbm, v_hbm))
    ]

    @pl.when(core == 0)
    def _():
        for copy in earl_copies + earl_locals:
            copy.start()

    def load_queries(head, carry):
        for g in range(GRP):
            query_load(head, g).start()
        return carry

    lax.fori_loop(0, KVH, load_queries, 0)

    def wait_cache(head, carry):
        for copy in cache_loads(head):
            copy.wait()
        return carry

    lax.fori_loop(0, KVH, wait_cache, 0)

    def pk_wait(k, carry):
        pk_copy(k).wait_recv()
        return carry

    lax.fori_loop(1, n, pk_wait, 0)
    to_scalar = pltpu.make_async_copy(pk, pk_sm, sm_sem.at[0])
    to_scalar.start()
    to_scalar.wait()

    def served(k, pair):
        found = [(jnp.int32(0), jnp.int32(0))] * slots
        count = jnp.int32(0)
        for e in range(WANTED):
            block = pk_sm[k, 0, e]
            match = lax.rem(block, n) == pair
            for m in range(slots):
                hit = match & (count == m)
                head, row = found[m]
                found[m] = (jnp.where(hit, e % KVH, head), jnp.where(hit, lax.div(block, n), row))
            count = count + match.astype(jnp.int32)
        return found

    def gather(k, dst):
        for m, (head, row) in enumerate(served(k, chip)):
            dst[m, 0] = kv[row * KVH + head]
            dst[m, 1] = vv[row * KVH + head]

    def a2a_copy(k):
        return remote(send.at[k], recv.at[k, core], a2a_s.at[k], a2a_r.at[k], peer(k))

    def a2a_send(i, carry):
        k = n - 1 - i
        gather(k, send.at[k])
        a2a_copy(k).start()
        return carry

    for ch in range(CHUNKS):
        @pl.when(column & (chip != 0))
        def _():
            blk_copy(0, ch).wait_recv()
            blk_start(ch)

        a2a_send(ch, 0)

    lax.fori_loop(CHUNKS, n - 1, a2a_send, 0)
    gather(0, recv.at[0, core])

    def fwd_copy(k):
        return remote(recv.at[k, core], recv.at[k, core], fwd_s.at[k], fwd_r.at[k], sibling)

    fwd_copy(0).start()

    @pl.when(jnp.logical_not(column) & (chip != 0))
    def _():
        for ch in range(CHUNKS):
            blk_copy(0, ch).wait_recv()
            blk_start(ch)

    def wait_queries(head, carry):
        for g in range(GRP):
            query_load(head, g).wait()
        return carry

    lax.fori_loop(0, KVH, wait_queries, 0)

    @pl.when(core == 0)
    def _():
        for copy in earl_locals:
            copy.wait()

    @pl.when(core == 1)
    def _():
        for copy in earl_copies:
            copy.wait_recv()

    def picked(k):
        for m, (head, _) in enumerate(served(0, xor_of(chip, k, n))):
            keys = jnp.concatenate([recv[k, 0, m, 0], recv[k, 1, m, 0]], axis=0)
            values = jnp.concatenate([recv[k, 0, m, 1], recv[k, 1, m, 1]], axis=0)
            blended, highest, total = partial_attend(qv[head], keys, values)
            acc_p[k * slots + m] = blended
            max_p[k * slots + m] = highest
            tot_p[k * slots + m] = total

    def forward(k):
        a2a_copy(k).wait_recv()
        fwd_copy(k).start()

    def sib_wait(k):
        remote(
            recv.at[k, 1 - core], recv.at[k, 1 - core], fwd_s.at[k], fwd_r.at[k], sibling
        ).wait_recv()

    sib_wait(0)
    picked(0)

    for ch in range(CHUNKS):
        blk_sib(ch).wait_recv()

    def local_head(head, carry):
        window = pl.ds(pl.multiple_of(head * HD, HD), HD)
        keys = jnp.concatenate(
            [blk[0, 0, :, window], blk[1, 0, :, window], earl[0, :, window], kv[last * KVH + head]], axis=0
        )
        values = jnp.concatenate(
            [blk[0, 1, :, window], blk[1, 1, :, window], earl[1, :, window], vv[last * KVH + head]], axis=0
        )
        shape = (GRP * half, 4 * half)
        columns = lax.broadcasted_iota(jnp.int32, shape, 1)
        query_pos = lax.broadcasted_iota(jnp.int32, shape, 0) % half
        usable = columns < 2 * half + half * core
        usable = usable | ((columns >= 3 * half) & (columns - 3 * half <= query_pos))
        blended, highest, total = partial_attend(qv[head], keys, values, usable)
        acc_l[head] = blended
        max_l[head] = highest
        tot_l[head] = total
        return carry

    lax.fori_loop(0, KVH, local_head, 0)

    def step(i, carry):
        k = n - i
        forward(n - 1 - i)
        sib_wait(k)
        picked(k)
        return carry

    forward(n - 1)
    lax.fori_loop(1, n - 1, step, 0)
    sib_wait(1)
    picked(1)

    def out_copy(head):
        window = pl.ds(pl.multiple_of(head * GRP * HD, GRP * HD), GRP * HD)
        return pltpu.make_async_copy(stage.at[:, window], o_hbm.at[:, window], out_sem.at[head])

    def merge(head, carry):
        parts = [(acc_l[head], max_l[head], tot_l[head])]
        for s in range(FURTHER):
            entry = s * KVH + head
            pair = lax.rem(pk_sm[0, 0, entry], n)
            rank = jnp.int32(0)
            for e in range(WANTED):
                same = (lax.rem(pk_sm[0, 0, e], n) == pair) & (e < entry)
                rank = rank + same.astype(jnp.int32)
            index = xor_of(pair, chip, n) * slots + jnp.minimum(rank, slots - 1)
            parts.append((acc_p[index], max_p[index], tot_p[index]))
        top = functools.reduce(jnp.maximum, [part[1] for part in parts])
        shares = [jnp.exp2((part[1] - top) * EXP2_SCALE) for part in parts]
        total = sum(share * part[2] for share, part in zip(shares, parts))
        result = sum((share / total) * part[0] for share, part in zip(shares, parts))
        result = result.astype(stage.dtype)
        for g in range(GRP):
            window = pl.ds(pl.multiple_of((head * GRP + g) * HD, HD), HD)
            stage[:, window] = result[g * half:(g + 1) * half]
        out_copy(head).start()
        return carry

    lax.fori_loop(0, KVH, merge, 0)

    def drain(k, carry):
        pk_copy(k).wait_send()
        a2a_copy(k).wait_send()
        return carry

    lax.fori_loop(1, n, drain, 0)

    def drain_fwd(k, carry):
        fwd_copy(k).wait_send()
        return carry

    lax.fori_loop(0, n, drain_fwd, 0)
    for ch in range(CHUNKS):
        for kind, (wanted, _) in enumerate(routes):
            @pl.when(wanted)
            def _():
                blk_copy(kind, ch).wait_send()
        blk_sib(ch).wait_send()

    @pl.when(core == 0)
    def _():
        for copy in earl_copies:
            copy.wait_send()

    def drain_out(head, carry):
        out_copy(head).wait()
        return carry

    lax.fori_loop(0, KVH, drain_out, 0)


def solution(mesh):
    n = mesh.shape["ctx"] // 2
    slots = (WANTED + n - 1) // n
    bf16, f32 = jnp.bfloat16, jnp.float32

    def shard(queries, keys, values, picks):
        half, width = queries.shape
        rows = keys.shape[0]
        kv_width = keys.shape[2]
        dma = pltpu.SemaphoreType.DMA
        anywhere = pl.BlockSpec(memory_space=pl.ANY)
        return pl.pallas_call(
            functools.partial(kernel, n, slots),
            out_shape=jax.ShapeDtypeStruct(queries.shape, bf16),
            in_specs=[anywhere, anywhere, anywhere, anywhere],
            out_specs=anywhere,
            scratch_shapes=[
                pltpu.VMEM(picks.shape, jnp.int32),
                pltpu.VMEM((KVH, GRP * half, HD), bf16),
                pltpu.VMEM((rows * KVH, half, HD), bf16),
                pltpu.VMEM((rows * KVH, half, HD), bf16),
                pltpu.VMEM((2, 2, half, kv_width), bf16),
                pltpu.VMEM((2, half, kv_width), bf16),
                pltpu.VMEM((n, 1, HD), jnp.int32),
                pltpu.SMEM((n, 1, HD), jnp.int32),
                pltpu.VMEM((n, slots, 2, half, HD), bf16),
                pltpu.VMEM((n, 2, slots, 2, half, HD), bf16),
                pltpu.VMEM((KVH, GRP * half, HD), f32),
                pltpu.VMEM((KVH, GRP * half, 1), f32),
                pltpu.VMEM((KVH, GRP * half, 1), f32),
                pltpu.VMEM((n * slots, GRP * half, HD), f32),
                pltpu.VMEM((n * slots, GRP * half, 1), f32),
                pltpu.VMEM((n * slots, GRP * half, 1), f32),
                pltpu.VMEM((half, width), bf16),
                dma((2, rows, KVH)), dma((KVH, GRP)), dma((2,)), dma((2,)), dma((2,)), dma((2,)),
                dma((n,)), dma((n,)), dma((2,)),
                dma((6, CHUNKS)), dma((2, CHUNKS)),
                dma((n,)), dma((n,)), dma((n,)), dma((n,)), dma((KVH,)),
            ],
            compiler_params=pltpu.CompilerParams(
                collective_id=0, has_side_effects=True, vmem_limit_bytes=56 * 2**20
            ),
        )(picks, queries, keys, values)

    placed = (
        P(("groups", "ctx"), None),
        P(None, ("groups", "ctx"), None),
        P(None, ("groups", "ctx"), None),
        P(("groups", "ctx"), None, None),
    )
    return jax.shard_map(
        shard, mesh=mesh, in_specs=placed, out_specs=P(("groups", "ctx"), None), check_vma=False
    )
```

```python
import functools
import math

import jax
import jax.numpy as jnp
from jax import lax
from jax.experimental import pallas as pl
from jax.experimental.pallas import tpu as pltpu
from jax.sharding import PartitionSpec as P

HD = 128
KVH = 8
GRP = 4
FURTHER = 2
WANTED = KVH * FURTHER
CHUNKS = 4
MESH = pl.DeviceIdType.MESH
SCALE = HD ** -0.5
EXP2_SCALE = SCALE * math.log2(math.e)


def xor_of(a, b, n):
    a, b = jnp.int32(a), jnp.int32(b)
    total = 0
    bit = 1
    while bit < n:
        total = total + lax.rem(lax.rem(lax.div(a, bit), 2) + lax.rem(lax.div(b, bit), 2), 2) * bit
        bit *= 2
    return total


def partial_attend(rows, keys, values, usable=None):
    scores = lax.dot_general(
        rows, keys, (((1,), (1,)), ((), ())), preferred_element_type=jnp.float32
    )
    if usable is not None:
        scores = jnp.where(usable, scores, -jnp.inf)
    highest = jnp.max(scores, axis=-1, keepdims=True)
    weights = jnp.exp2((scores - highest) * EXP2_SCALE)
    total = jnp.sum(weights, axis=-1, keepdims=True)
    blended = jnp.dot(
        weights.astype(jnp.bfloat16), values, preferred_element_type=jnp.float32
    )
    return blended, highest, total


def kernel(
    n, slots, picks_hbm, q_hbm, k_hbm, v_hbm, o_hbm,
    own_picks, qv, kv, vv, blk, earl, pk, pk_sm, send, recv,
    acc_l, max_l, tot_l, acc_p, max_p, tot_p, stage,
    load_sem, q_sem, root_sem, earl_loc, earl_s, earl_r, pk_s, pk_r, sm_sem,
    blk_s, blk_r, a2a_s, a2a_r, fwd_s, fwd_r, out_sem,
):
    me = lax.axis_index("ctx")
    chip, core = me // 2, me % 2
    z, y = chip // 2, chip % 2
    depth = n // 2
    half = q_hbm.shape[0]
    last = k_hbm.shape[0] - 1
    sibling = chip * 2 + 1 - core

    def peer(k):
        return xor_of(chip, k, n) * 2 + core

    def remote(src, dst, s_sem, r_sem, dest):
        return pltpu.make_async_remote_copy(
            src_ref=src, dst_ref=dst, send_sem=s_sem, recv_sem=r_sem,
            device_id={"ctx": dest}, device_id_type=MESH,
        )

    def cache_loads(head):
        window = pl.ds(pl.multiple_of(head * HD, HD), HD)
        return [
            pltpu.make_async_copy(src.at[:, :, window], dst.at[head], load_sem.at[i, head])
            for i, (src, dst) in enumerate(((k_hbm, kv), (v_hbm, vv)))
        ]

    def query_load(head, g):
        window = pl.ds(pl.multiple_of((head * GRP + g) * HD, HD), HD)
        return pltpu.make_async_copy(q_hbm.at[:, window], qv.at[head, pl.ds(g * half, half)], q_sem.at[head, g])

    root_loads = [
        pltpu.make_async_copy(src.at[0], blk.at[core, i], root_sem.at[i])
        for i, src in enumerate((k_hbm, v_hbm))
    ]

    picks_load = pltpu.make_async_copy(picks_hbm, own_picks, sm_sem.at[1])
    picks_load.start()

    @pl.when(chip == 0)
    def _():
        for copy in root_loads:
            copy.start()

    def load_cache(head, carry):
        for copy in cache_loads(head):
            copy.start()
        return carry

    lax.fori_loop(0, KVH, load_cache, 0)

    barrier = pltpu.get_barrier_semaphore()

    def greet(k, carry):
        pl.semaphore_signal(barrier, inc=1, device_id={"ctx": peer(k)}, device_id_type=MESH)
        return carry

    lax.fori_loop(1, n, greet, 0)
    pl.semaphore_signal(barrier, inc=1, device_id={"ctx": sibling}, device_id_type=MESH)

    lanes = lax.broadcasted_iota(jnp.int32, (KVH, HD), 1)
    subs = lax.broadcasted_iota(jnp.int32, (KVH, HD), 0)
    picks_load.wait()
    mine = own_picks[0]
    spread = jnp.where(lanes == subs, mine[:, 0:1], 0)
    spread = spread + jnp.where(lanes == subs + KVH, mine[:, 1:2], 0)
    pk[0] = jnp.sum(spread, axis=0, keepdims=True)

    pl.semaphore_wait(barrier, n)

    def pk_copy(k):
        return remote(pk.at[0], pk.at[k], pk_s.at[k], pk_r.at[k], peer(k))

    def pk_send(k, carry):
        pk_copy(k).start()
        return carry

    lax.fori_loop(1, n, pk_send, 0)

    rows_of = half // (CHUNKS // 2)

    def blk_part(side, ch):
        return blk.at[side, ch // (CHUNKS // 2), pl.ds((ch % (CHUNKS // 2)) * rows_of, rows_of)]

    column = y == core
    routes = [
        (column & (z + 1 < depth), ((z + 1) * 2 + y) * 2 + core),
        (column & jnp.logical_not((core == 1) & (z == 0)), (z * 2 + 1 - y) * 2 + core),
        ((chip == 0) & (core == 1), 3),
    ]

    def blk_copy(kind, ch):
        return remote(
            blk_part(core, ch), blk_part(core, ch), blk_s.at[kind, ch], blk_r.at[0, ch], routes[kind][1]
        )

    def blk_sib(ch):
        return remote(
            blk_part(core, ch), blk_part(core, ch), blk_s.at[len(routes), ch], blk_r.at[1, ch], sibling
        )

    def blk_start(ch):
        for kind, (wanted, _) in enumerate(routes):
            @pl.when(wanted)
            def _():
                blk_copy(kind, ch).start()
        blk_sib(ch).start()

    @pl.when(chip == 0)
    def _():
        for copy in root_loads:
            copy.wait()
        for ch in range(CHUNKS):
            blk_start(ch)

    earl_copies = [
        remote(src.at[last], earl.at[i], earl_s.at[i], earl_r.at[i], sibling)
        for i, src in enumerate((k_hbm, v_hbm))
    ]
    earl_locals = [
        pltpu.make_async_copy(src.at[last], earl.at[i], earl_loc.at[i])
        for i, src in enumerate((k_hbm, v_hbm))
    ]

    @pl.when(core == 0)
    def _():
        for copy in earl_copies + earl_locals:
            copy.start()

    def load_queries(head, carry):
        for g in range(GRP):
            query_load(head, g).start()
        return carry

    def wait_cache(head, carry):
        for copy in cache_loads(head):
            copy.wait()
        return carry

    def pk_wait(k, carry):
        pk_copy(k).wait_recv()
        return carry

    early = column & (chip != 0) & (z <= 1)

    @pl.when(early)
    def _():
        for ch in range(2):
            blk_copy(0, ch).wait_recv()
            blk_start(ch)

    lax.fori_loop(1, n, pk_wait, 0)
    to_scalar = pltpu.make_async_copy(pk, pk_sm, sm_sem.at[0])
    to_scalar.start()
    lax.fori_loop(0, KVH, wait_cache, 0)
    to_scalar.wait()

    def served(k, pair):
        found = [(jnp.int32(0), jnp.int32(0))] * slots
        count = jnp.int32(0)
        for e in range(WANTED):
            block = pk_sm[k, 0, e]
            match = lax.rem(block, n) == pair
            for m in range(slots):
                hit = match & (count == m)
                head, row = found[m]
                found[m] = (jnp.where(hit, e % KVH, head), jnp.where(hit, lax.div(block, n), row))
            count = count + match.astype(jnp.int32)
        return found

    def gather(k, dst):
        for m, (head, row) in enumerate(served(k, chip)):
            dst[m, 0] = kv[head, row]
            dst[m, 1] = vv[head, row]

    def a2a_copy(k):
        return remote(send.at[k], recv.at[k, core], a2a_s.at[k], a2a_r.at[k], peer(k))

    def a2a_send(i, carry):
        k = n - 1 - i
        gather(k, send.at[k])
        a2a_copy(k).start()
        return carry

    for ch in range(CHUNKS):
        @pl.when(column & (chip != 0) & ((z > 1) | (ch >= 2)))
        def _():
            blk_copy(0, ch).wait_recv()
            blk_start(ch)

        a2a_send(ch, 0)

    lax.fori_loop(CHUNKS, n - 1, a2a_send, 0)
    gather(0, recv.at[0, core])

    def fwd_copy(k):
        return remote(recv.at[k, core], recv.at[k, core], fwd_s.at[k], fwd_r.at[k], sibling)

    fwd_copy(0).start()
    lax.fori_loop(0, KVH, load_queries, 0)

    @pl.when(jnp.logical_not(column) & (chip != 0))
    def _():
        for ch in range(CHUNKS):
            blk_copy(0, ch).wait_recv()
            blk_start(ch)

    def wait_queries(head, carry):
        for g in range(GRP):
            query_load(head, g).wait()
        return carry

    lax.fori_loop(0, KVH, wait_queries, 0)

    @pl.when(core == 0)
    def _():
        for copy in earl_locals:
            copy.wait()

    @pl.when(core == 1)
    def _():
        for copy in earl_copies:
            copy.wait_recv()

    def picked(k):
        for m, (head, _) in enumerate(served(0, xor_of(chip, k, n))):
            keys = jnp.concatenate([recv[k, 0, m, 0], recv[k, 1, m, 0]], axis=0)
            values = jnp.concatenate([recv[k, 0, m, 1], recv[k, 1, m, 1]], axis=0)
            blended, highest, total = partial_attend(qv[head], keys, values)
            acc_p[k * slots + m] = blended
            max_p[k * slots + m] = highest
            tot_p[k * slots + m] = total

    def forward(k):
        a2a_copy(k).wait_recv()
        fwd_copy(k).start()

    def sib_wait(k):
        remote(
            recv.at[k, 1 - core], recv.at[k, 1 - core], fwd_s.at[k], fwd_r.at[k], sibling
        ).wait_recv()

    sib_wait(0)
    picked(0)

    for ch in range(CHUNKS):
        blk_sib(ch).wait_recv()

    def local_head(head, carry):
        window = pl.ds(pl.multiple_of(head * HD, HD), HD)
        keys = jnp.concatenate(
            [blk[0, 0, :, window], blk[1, 0, :, window], earl[0, :, window], kv[head, last]], axis=0
        )
        values = jnp.concatenate(
            [blk[0, 1, :, window], blk[1, 1, :, window], earl[1, :, window], vv[head, last]], axis=0
        )
        shape = (GRP * half, 4 * half)
        columns = lax.broadcasted_iota(jnp.int32, shape, 1)
        query_pos = lax.broadcasted_iota(jnp.int32, shape, 0) % half
        usable = columns < 2 * half + half * core
        usable = usable | ((columns >= 3 * half) & (columns - 3 * half <= query_pos))
        blended, highest, total = partial_attend(qv[head], keys, values, usable)
        acc_l[head] = blended
        max_l[head] = highest
        tot_l[head] = total
        return carry

    lax.fori_loop(0, KVH, local_head, 0)

    def step(i, carry):
        k = n - i
        forward(n - 1 - i)
        sib_wait(k)
        picked(k)
        return carry

    forward(n - 1)
    lax.fori_loop(1, n - 1, step, 0)
    sib_wait(1)
    picked(1)

    def out_copy(head):
        window = pl.ds(pl.multiple_of(head * GRP * HD, GRP * HD), GRP * HD)
        return pltpu.make_async_copy(stage.at[:, window], o_hbm.at[:, window], out_sem.at[head])

    def merge(head, carry):
        parts = [(acc_l[head], max_l[head], tot_l[head])]
        for s in range(FURTHER):
            entry = s * KVH + head
            pair = lax.rem(pk_sm[0, 0, entry], n)
            rank = jnp.int32(0)
            for e in range(WANTED):
                same = (lax.rem(pk_sm[0, 0, e], n) == pair) & (e < entry)
                rank = rank + same.astype(jnp.int32)
            index = xor_of(pair, chip, n) * slots + jnp.minimum(rank, slots - 1)
            parts.append((acc_p[index], max_p[index], tot_p[index]))
        top = functools.reduce(jnp.maximum, [part[1] for part in parts])
        shares = [jnp.exp2((part[1] - top) * EXP2_SCALE) for part in parts]
        total = sum(share * part[2] for share, part in zip(shares, parts))
        result = sum((share / total) * part[0] for share, part in zip(shares, parts))
        result = result.astype(stage.dtype)
        for g in range(GRP):
            window = pl.ds(pl.multiple_of((head * GRP + g) * HD, HD), HD)
            stage[:, window] = result[g * half:(g + 1) * half]
        out_copy(head).start()
        return carry

    lax.fori_loop(0, KVH, merge, 0)

    def drain(k, carry):
        pk_copy(k).wait_send()
        a2a_copy(k).wait_send()
        return carry

    lax.fori_loop(1, n, drain, 0)

    def drain_fwd(k, carry):
        fwd_copy(k).wait_send()
        return carry

    lax.fori_loop(0, n, drain_fwd, 0)
    for ch in range(CHUNKS):
        for kind, (wanted, _) in enumerate(routes):
            @pl.when(wanted)
            def _():
                blk_copy(kind, ch).wait_send()
        blk_sib(ch).wait_send()

    @pl.when(core == 0)
    def _():
        for copy in earl_copies:
            copy.wait_send()

    def drain_out(head, carry):
        out_copy(head).wait()
        return carry

    lax.fori_loop(0, KVH, drain_out, 0)


def solution(mesh):
    n = mesh.shape["ctx"] // 2
    slots = (WANTED + n - 1) // n
    bf16, f32 = jnp.bfloat16, jnp.float32

    def shard(queries, keys, values, picks):
        half, width = queries.shape
        rows = keys.shape[0]
        kv_width = keys.shape[2]
        dma = pltpu.SemaphoreType.DMA
        anywhere = pl.BlockSpec(memory_space=pl.ANY)
        return pl.pallas_call(
            functools.partial(kernel, n, slots),
            out_shape=jax.ShapeDtypeStruct(queries.shape, bf16),
            in_specs=[anywhere, anywhere, anywhere, anywhere],
            out_specs=anywhere,
            scratch_shapes=[
                pltpu.VMEM(picks.shape, jnp.int32),
                pltpu.VMEM((KVH, GRP * half, HD), bf16),
                pltpu.VMEM((KVH, rows, half, HD), bf16),
                pltpu.VMEM((KVH, rows, half, HD), bf16),
                pltpu.VMEM((2, 2, half, kv_width), bf16),
                pltpu.VMEM((2, half, kv_width), bf16),
                pltpu.VMEM((n, 1, HD), jnp.int32),
                pltpu.SMEM((n, 1, HD), jnp.int32),
                pltpu.VMEM((n, slots, 2, half, HD), bf16),
                pltpu.VMEM((n, 2, slots, 2, half, HD), bf16),
                pltpu.VMEM((KVH, GRP * half, HD), f32),
                pltpu.VMEM((KVH, GRP * half, 1), f32),
                pltpu.VMEM((KVH, GRP * half, 1), f32),
                pltpu.VMEM((n * slots, GRP * half, HD), f32),
                pltpu.VMEM((n * slots, GRP * half, 1), f32),
                pltpu.VMEM((n * slots, GRP * half, 1), f32),
                pltpu.VMEM((half, width), bf16),
                dma((2, KVH)), dma((KVH, GRP)), dma((2,)), dma((2,)), dma((2,)), dma((2,)),
                dma((n,)), dma((n,)), dma((2,)),
                dma((6, CHUNKS)), dma((2, CHUNKS)),
                dma((n,)), dma((n,)), dma((n,)), dma((n,)), dma((KVH,)),
            ],
            compiler_params=pltpu.CompilerParams(
                collective_id=0, has_side_effects=True, vmem_limit_bytes=56 * 2**20
            ),
        )(picks, queries, keys, values)

    placed = (
        P(("groups", "ctx"), None),
        P(None, ("groups", "ctx"), None),
        P(None, ("groups", "ctx"), None),
        P(("groups", "ctx"), None, None),
    )
    return jax.shard_map(
        shard, mesh=mesh, in_specs=placed, out_specs=P(("groups", "ctx"), None), check_vma=False
    )
```

```python
import functools
import math

import jax
import jax.numpy as jnp
from jax import lax
from jax.experimental import pallas as pl
from jax.experimental.pallas import tpu as pltpu
from jax.sharding import PartitionSpec as P

HD = 128
KVH = 8
GRP = 4
FURTHER = 2
WANTED = KVH * FURTHER
CHUNKS = 4
MESH = pl.DeviceIdType.MESH
SCALE = HD ** -0.5
EXP2_SCALE = SCALE * math.log2(math.e)


def xor_of(a, b, n):
    a, b = jnp.int32(a), jnp.int32(b)
    total = 0
    bit = 1
    while bit < n:
        total = total + lax.rem(lax.rem(lax.div(a, bit), 2) + lax.rem(lax.div(b, bit), 2), 2) * bit
        bit *= 2
    return total


def partial_attend(rows, keys, values, usable=None):
    scores = lax.dot_general(
        rows, keys, (((1,), (1,)), ((), ())), preferred_element_type=jnp.float32
    )
    if usable is not None:
        scores = jnp.where(usable, scores, -jnp.inf)
    highest = jnp.max(scores, axis=-1, keepdims=True)
    weights = jnp.exp2((scores - highest) * EXP2_SCALE)
    total = jnp.sum(weights, axis=-1, keepdims=True)
    blended = jnp.dot(
        weights.astype(jnp.bfloat16), values, preferred_element_type=jnp.float32
    )
    return blended, highest, total


def kernel(
    n, slots, picks_hbm, q_hbm, k_hbm, v_hbm, o_hbm,
    own_picks, qv, kv, vv, blk, earl, pk, pk_sm, send, recv,
    acc_l, max_l, tot_l, acc_p, max_p, tot_p, stage,
    load_sem, q_sem, root_sem, earl_loc, earl_s, earl_r, pk_s, pk_r, sm_sem,
    blk_s, blk_r, a2a_s, a2a_r, fwd_s, fwd_r, out_sem,
):
    me = lax.axis_index("ctx")
    chip, core = me // 2, me % 2
    z, y = chip // 2, chip % 2
    depth = n // 2
    half = q_hbm.shape[0]
    last = k_hbm.shape[0] - 1
    sibling = chip * 2 + 1 - core

    def peer(k):
        return xor_of(chip, k, n) * 2 + core

    def remote(src, dst, s_sem, r_sem, dest):
        return pltpu.make_async_remote_copy(
            src_ref=src, dst_ref=dst, send_sem=s_sem, recv_sem=r_sem,
            device_id={"ctx": dest}, device_id_type=MESH,
        )

    def cache_loads(head):
        window = pl.ds(pl.multiple_of(head * HD, HD), HD)
        return [
            pltpu.make_async_copy(src.at[:, :, window], dst.at[head], load_sem.at[i, head])
            for i, (src, dst) in enumerate(((k_hbm, kv), (v_hbm, vv)))
        ]

    def query_load(head, g):
        window = pl.ds(pl.multiple_of((head * GRP + g) * HD, HD), HD)
        return pltpu.make_async_copy(q_hbm.at[:, window], qv.at[head, pl.ds(g * half, half)], q_sem.at[head, g])

    root_loads = [
        pltpu.make_async_copy(src.at[0], blk.at[core, i], root_sem.at[i])
        for i, src in enumerate((k_hbm, v_hbm))
    ]

    picks_load = pltpu.make_async_copy(picks_hbm, own_picks, sm_sem.at[1])
    picks_load.start()

    @pl.when(chip == 0)
    def _():
        for copy in root_loads:
            copy.start()

    def load_cache(head, carry):
        for copy in cache_loads(head):
            copy.start()
        return carry

    lax.fori_loop(0, KVH, load_cache, 0)

    barrier = pltpu.get_barrier_semaphore()

    def greet(k, carry):
        pl.semaphore_signal(barrier, inc=1, device_id={"ctx": peer(k)}, device_id_type=MESH)
        return carry

    lax.fori_loop(1, n, greet, 0)
    pl.semaphore_signal(barrier, inc=1, device_id={"ctx": sibling}, device_id_type=MESH)

    lanes = lax.broadcasted_iota(jnp.int32, (KVH, HD), 1)
    subs = lax.broadcasted_iota(jnp.int32, (KVH, HD), 0)
    picks_load.wait()
    mine = own_picks[0]
    spread = jnp.where(lanes == subs, mine[:, 0:1], 0)
    spread = spread + jnp.where(lanes == subs + KVH, mine[:, 1:2], 0)
    pk[0] = jnp.sum(spread, axis=0, keepdims=True)

    pl.semaphore_wait(barrier, n)

    def pk_copy(k):
        return remote(pk.at[0], pk.at[k], pk_s.at[k], pk_r.at[k], peer(k))

    def pk_send(k, carry):
        pk_copy(k).start()
        return carry

    lax.fori_loop(1, n, pk_send, 0)

    rows_of = half // (CHUNKS // 2)

    def blk_part(side, ch):
        return blk.at[side, ch // (CHUNKS // 2), pl.ds((ch % (CHUNKS // 2)) * rows_of, rows_of)]

    column = y == core
    routes = [
        (column & (z == 0), (far * 2 + y) * 2 + core) for far in range(depth - 1, 0, -1)
    ] + [
        (column & jnp.logical_not((core == 1) & (z == 0)), (z * 2 + 1 - y) * 2 + core),
        ((chip == 0) & (core == 1), 3),
    ]

    def blk_copy(kind, ch):
        return remote(
            blk_part(core, ch), blk_part(core, ch), blk_s.at[kind, ch], blk_r.at[0, ch], routes[kind][1]
        )

    def blk_sib(ch):
        return remote(
            blk_part(core, ch), blk_part(core, ch), blk_s.at[len(routes), ch], blk_r.at[1, ch], sibling
        )

    def blk_start(ch):
        for kind, (wanted, _) in enumerate(routes):
            @pl.when(wanted)
            def _():
                blk_copy(kind, ch).start()
        blk_sib(ch).start()

    @pl.when(chip == 0)
    def _():
        for copy in root_loads:
            copy.wait()
        for ch in range(CHUNKS):
            blk_start(ch)

    earl_copies = [
        remote(src.at[last], earl.at[i], earl_s.at[i], earl_r.at[i], sibling)
        for i, src in enumerate((k_hbm, v_hbm))
    ]
    earl_locals = [
        pltpu.make_async_copy(src.at[last], earl.at[i], earl_loc.at[i])
        for i, src in enumerate((k_hbm, v_hbm))
    ]

    @pl.when(core == 0)
    def _():
        for copy in earl_copies + earl_locals:
            copy.start()

    def load_queries(head, carry):
        for g in range(GRP):
            query_load(head, g).start()
        return carry

    def wait_cache(head, carry):
        for copy in cache_loads(head):
            copy.wait()
        return carry

    def pk_wait(k, carry):
        pk_copy(k).wait_recv()
        return carry

    early = column & (chip != 0) & (z == 0)

    @pl.when(early)
    def _():
        for ch in range(2):
            blk_copy(0, ch).wait_recv()
            blk_start(ch)

    lax.fori_loop(1, n, pk_wait, 0)
    to_scalar = pltpu.make_async_copy(pk, pk_sm, sm_sem.at[0])
    to_scalar.start()
    lax.fori_loop(0, KVH, wait_cache, 0)
    to_scalar.wait()

    def served(k, pair):
        found = [(jnp.int32(0), jnp.int32(0))] * slots
        count = jnp.int32(0)
        for e in range(WANTED):
            block = pk_sm[k, 0, e]
            match = lax.rem(block, n) == pair
            for m in range(slots):
                hit = match & (count == m)
                head, row = found[m]
                found[m] = (jnp.where(hit, e % KVH, head), jnp.where(hit, lax.div(block, n), row))
            count = count + match.astype(jnp.int32)
        return found

    def gather(k, dst):
        for m, (head, row) in enumerate(served(k, chip)):
            dst[m, 0] = kv[head, row]
            dst[m, 1] = vv[head, row]

    def a2a_copy(k):
        return remote(send.at[k], recv.at[k, core], a2a_s.at[k], a2a_r.at[k], peer(k))

    def a2a_send(i, carry):
        k = n - 1 - i
        gather(k, send.at[k])
        a2a_copy(k).start()
        return carry

    for ch in range(CHUNKS):
        @pl.when(column & (chip != 0) & (z == 0) & (ch >= 2))
        def _():
            blk_copy(0, ch).wait_recv()
            blk_start(ch)

        a2a_send(ch, 0)

    lax.fori_loop(CHUNKS, n - 1, a2a_send, 0)
    gather(0, recv.at[0, core])

    def fwd_copy(k):
        return remote(recv.at[k, core], recv.at[k, core], fwd_s.at[k], fwd_r.at[k], sibling)

    fwd_copy(0).start()
    lax.fori_loop(0, KVH, load_queries, 0)

    @pl.when((jnp.logical_not(column) | (z > 0)) & (chip != 0))
    def _():
        for ch in range(CHUNKS):
            blk_copy(0, ch).wait_recv()
            blk_start(ch)

    def wait_queries(head, carry):
        for g in range(GRP):
            query_load(head, g).wait()
        return carry

    lax.fori_loop(0, KVH, wait_queries, 0)

    @pl.when(core == 0)
    def _():
        for copy in earl_locals:
            copy.wait()

    @pl.when(core == 1)
    def _():
        for copy in earl_copies:
            copy.wait_recv()

    def picked(k):
        for m, (head, _) in enumerate(served(0, xor_of(chip, k, n))):
            keys = jnp.concatenate([recv[k, 0, m, 0], recv[k, 1, m, 0]], axis=0)
            values = jnp.concatenate([recv[k, 0, m, 1], recv[k, 1, m, 1]], axis=0)
            blended, highest, total = partial_attend(qv[head], keys, values)
            acc_p[k * slots + m] = blended
            max_p[k * slots + m] = highest
            tot_p[k * slots + m] = total

    def forward(k):
        a2a_copy(k).wait_recv()
        fwd_copy(k).start()

    def sib_wait(k):
        remote(
            recv.at[k, 1 - core], recv.at[k, 1 - core], fwd_s.at[k], fwd_r.at[k], sibling
        ).wait_recv()

    sib_wait(0)
    picked(0)

    for ch in range(CHUNKS):
        blk_sib(ch).wait_recv()

    def local_head(head, carry):
        window = pl.ds(pl.multiple_of(head * HD, HD), HD)
        keys = jnp.concatenate(
            [blk[0, 0, :, window], blk[1, 0, :, window], earl[0, :, window], kv[head, last]], axis=0
        )
        values = jnp.concatenate(
            [blk[0, 1, :, window], blk[1, 1, :, window], earl[1, :, window], vv[head, last]], axis=0
        )
        shape = (GRP * half, 4 * half)
        columns = lax.broadcasted_iota(jnp.int32, shape, 1)
        query_pos = lax.broadcasted_iota(jnp.int32, shape, 0) % half
        usable = columns < 2 * half + half * core
        usable = usable | ((columns >= 3 * half) & (columns - 3 * half <= query_pos))
        blended, highest, total = partial_attend(qv[head], keys, values, usable)
        acc_l[head] = blended
        max_l[head] = highest
        tot_l[head] = total
        return carry

    lax.fori_loop(0, KVH, local_head, 0)

    def step(i, carry):
        k = n - i
        forward(n - 1 - i)
        sib_wait(k)
        picked(k)
        return carry

    forward(n - 1)
    lax.fori_loop(1, n - 1, step, 0)
    sib_wait(1)
    picked(1)

    def out_copy(head):
        window = pl.ds(pl.multiple_of(head * GRP * HD, GRP * HD), GRP * HD)
        return pltpu.make_async_copy(stage.at[:, window], o_hbm.at[:, window], out_sem.at[head])

    def merge(head, carry):
        parts = [(acc_l[head], max_l[head], tot_l[head])]
        for s in range(FURTHER):
            entry = s * KVH + head
            pair = lax.rem(pk_sm[0, 0, entry], n)
            rank = jnp.int32(0)
            for e in range(WANTED):
                same = (lax.rem(pk_sm[0, 0, e], n) == pair) & (e < entry)
                rank = rank + same.astype(jnp.int32)
            index = xor_of(pair, chip, n) * slots + jnp.minimum(rank, slots - 1)
            parts.append((acc_p[index], max_p[index], tot_p[index]))
        top = functools.reduce(jnp.maximum, [part[1] for part in parts])
        shares = [jnp.exp2((part[1] - top) * EXP2_SCALE) for part in parts]
        total = sum(share * part[2] for share, part in zip(shares, parts))
        result = sum((share / total) * part[0] for share, part in zip(shares, parts))
        result = result.astype(stage.dtype)
        for g in range(GRP):
            window = pl.ds(pl.multiple_of((head * GRP + g) * HD, HD), HD)
            stage[:, window] = result[g * half:(g + 1) * half]
        out_copy(head).start()
        return carry

    lax.fori_loop(0, KVH, merge, 0)

    def drain(k, carry):
        pk_copy(k).wait_send()
        a2a_copy(k).wait_send()
        return carry

    lax.fori_loop(1, n, drain, 0)

    def drain_fwd(k, carry):
        fwd_copy(k).wait_send()
        return carry

    lax.fori_loop(0, n, drain_fwd, 0)
    for ch in range(CHUNKS):
        for kind, (wanted, _) in enumerate(routes):
            @pl.when(wanted)
            def _():
                blk_copy(kind, ch).wait_send()
        blk_sib(ch).wait_send()

    @pl.when(core == 0)
    def _():
        for copy in earl_copies:
            copy.wait_send()

    def drain_out(head, carry):
        out_copy(head).wait()
        return carry

    lax.fori_loop(0, KVH, drain_out, 0)


def solution(mesh):
    n = mesh.shape["ctx"] // 2
    slots = (WANTED + n - 1) // n
    bf16, f32 = jnp.bfloat16, jnp.float32

    def shard(queries, keys, values, picks):
        half, width = queries.shape
        rows = keys.shape[0]
        kv_width = keys.shape[2]
        dma = pltpu.SemaphoreType.DMA
        anywhere = pl.BlockSpec(memory_space=pl.ANY)
        return pl.pallas_call(
            functools.partial(kernel, n, slots),
            out_shape=jax.ShapeDtypeStruct(queries.shape, bf16),
            in_specs=[anywhere, anywhere, anywhere, anywhere],
            out_specs=anywhere,
            scratch_shapes=[
                pltpu.VMEM(picks.shape, jnp.int32),
                pltpu.VMEM((KVH, GRP * half, HD), bf16),
                pltpu.VMEM((KVH, rows, half, HD), bf16),
                pltpu.VMEM((KVH, rows, half, HD), bf16),
                pltpu.VMEM((2, 2, half, kv_width), bf16),
                pltpu.VMEM((2, half, kv_width), bf16),
                pltpu.VMEM((n, 1, HD), jnp.int32),
                pltpu.SMEM((n, 1, HD), jnp.int32),
                pltpu.VMEM((n, slots, 2, half, HD), bf16),
                pltpu.VMEM((n, 2, slots, 2, half, HD), bf16),
                pltpu.VMEM((KVH, GRP * half, HD), f32),
                pltpu.VMEM((KVH, GRP * half, 1), f32),
                pltpu.VMEM((KVH, GRP * half, 1), f32),
                pltpu.VMEM((n * slots, GRP * half, HD), f32),
                pltpu.VMEM((n * slots, GRP * half, 1), f32),
                pltpu.VMEM((n * slots, GRP * half, 1), f32),
                pltpu.VMEM((half, width), bf16),
                dma((2, KVH)), dma((KVH, GRP)), dma((2,)), dma((2,)), dma((2,)), dma((2,)),
                dma((n,)), dma((n,)), dma((2,)),
                dma((n // 2 + 2, CHUNKS)), dma((2, CHUNKS)),
                dma((n,)), dma((n,)), dma((n,)), dma((n,)), dma((KVH,)),
            ],
            compiler_params=pltpu.CompilerParams(
                collective_id=0, has_side_effects=True, vmem_limit_bytes=56 * 2**20
            ),
        )(picks, queries, keys, values)

    placed = (
        P(("groups", "ctx"), None),
        P(None, ("groups", "ctx"), None),
        P(None, ("groups", "ctx"), None),
        P(("groups", "ctx"), None, None),
    )
    return jax.shard_map(
        shard, mesh=mesh, in_specs=placed, out_specs=P(("groups", "ctx"), None), check_vma=False
    )
```
